32 devices in a mesh: dp: 8 (over y, x, core), tensor: 4 (over z).
Axes of the slice: x: 2, y: 2, z: 4, core: 2. Of those that a mesh axis runs over, the one named last changes fastest.
Arguments:
- inputs: bfloat16 [24, 1024, 768], P('dp', 'tensor'), may hold values from -6 to 6
- cotangent: bfloat16 [24, 1024, 768], P('dp', 'tensor'), may hold values from -6 to 6
- w_qkv: bfloat16 [768, 3, 768], P('dp', None, 'tensor'), may hold values from -0.21875 to 0.21875
- b_qkv: bfloat16 [3, 768], P(None, 'dp'), may hold values from -3 to 3
- w_attn_out: bfloat16 [768, 768], P('tensor', 'dp'), may hold values from -1.75 to 1.75
- w_up: bfloat16 [768, 3072], P('dp', 'tensor'), may hold values from -0.21875 to 0.21875
- b_up: bfloat16 [3072], P('dp'), may hold values from -3 to 3
- w_down: bfloat16 [3072, 768], P('tensor', 'dp'), may hold values from -0.109375 to 0.109375
- vectors: bfloat16 [5, 768], P(None, 'dp'), may hold values from 0.25 to 1.75
Outputs:
- output: bfloat16 [24, 1024, 768], P('dp', 'tensor')
- grad_inputs: bfloat16 [24, 1024, 768], P('dp', 'tensor')
- grad_w_qkv: float32 [768, 3, 768], P('dp', None, 'tensor')
- grad_b_qkv: float32 [3, 768], P(None, 'dp')
- grad_w_attn_out: float32 [768, 768], P('tensor', 'dp')
- grad_w_up: float32 [768, 3072], P('dp', 'tensor')
- grad_b_up: float32 [3072], P('dp')
- grad_w_down: float32 [3072, 768], P('tensor', 'dp')
- grad_vectors: float32 [5, 768], P(None, 'dp')
The draws below stay inside these ranges and needn't reach their ends.
All inputs are finite; a program needn't handle non-finite values.
Results may differ from the reference program's by a relative error of at most 0.012.
The reference program's roundings to bfloat16 on the way count: a program that leaves them out, or rounds other values in their place, can miss the bound.
Values may be sent and summed in bfloat16 or wider, within the bound.
A program may use at most 128 MiB of HBM per device.

```python
import jax
import jax.numpy as jnp
from jax import lax

D = 768
HEADS = 12
HD = 64
ROT = 16
FF = 3072
LEN = 1024
SEQS = 24


def strengthened(array, own_key, source, target, shards_of, factor):
    def block_of(position):
        return (jnp.arange(array.shape[position]) // (array.shape[position] // shards_of)).reshape((-1,) + (1,) * (array.ndim - 1 - position))

    near = jax.random.permutation(own_key, shards_of)[block_of(target)]
    other_side = (block_of(target) + shards_of // 2) % shards_of
    return jnp.where((block_of(source) == near) | (block_of(source) == other_side), factor * array, array)


def level_of(stream_key, dims, split, low, high):
    def one(axis_at, blocks):
        draws = jax.random.uniform(jax.random.fold_in(jax.random.fold_in(stream_key, 6), axis_at), (blocks,), jnp.float32, low / len(split), high / len(split))
        return jnp.repeat(jnp.exp(draws), dims[axis_at] // blocks).reshape((-1,) + (1,) * (len(dims) - axis_at - 1))

    loudness = one(*split[0])
    for cut in split[1:]:
        loudness = loudness * one(*cut)
    return loudness


def noise(stream_key, dims, width, most, shards=(), held_as=jnp.bfloat16):
    loudness = level_of(stream_key, dims, shards, -0.22, 0.18) if shards else 1.0
    values = jax.random.normal(stream_key, dims, jnp.float32) * width * loudness
    return jnp.minimum(jnp.maximum(values, -most), most).astype(held_as)


def gaussian_with(key, shape, deviation, most, shards, heavy, kind=jnp.bfloat16):
    values = deviation * jax.random.normal(key, shape, jnp.float32)
    if shards:
        values = values * level_of(key, shape, shards, -0.22, 0.18)
    return jnp.clip(strengthened(values, jax.random.fold_in(key, 3), *heavy), -most, most).astype(kind)


def setup_inputs(seed: int = 0) -> dict:
    key_of = jax.random.split(jax.random.key(seed), 10)
    return {
        "inputs": gaussian_with(key_of[0], (SEQS, LEN, D), 1.0, 6.0, ((0, 8), (1, 4)), (0, 2, 8, 2.0)),
        "cotangent": gaussian_with(key_of[1], (SEQS, LEN, D), 1.0, 6.0, ((0, 8), (1, 4)), (0, 2, 8, 2.0)),
        "w_qkv": noise(key_of[2], (D, 3, D), D ** -0.5, 0.21875, ((0, 8), (2, 4))),
        "b_qkv": noise(key_of[3], (3, D), 0.5, 3.0, ((1, 8),)),
        "w_attn_out": noise(key_of[4], (D, D), (max(D // 64, 1)) ** -0.5, 1.75, ((0, 4), (1, 8))),
        "w_up": noise(key_of[5], (D, FF), D ** -0.5, 0.21875, ((0, 8), (1, 4))),
        "b_up": noise(key_of[6], (FF,), 0.5, 3.0, ((0, 8),)),
        "w_down": noise(key_of[7], (FF, D), FF ** -0.5, 0.109375, ((0, 4), (1, 8))),
        "vectors": jnp.clip(1.0 + 0.15 * jax.random.normal(key_of[8], (5, D), jnp.float32), 0.25, 1.75).astype(jnp.bfloat16),
    }


@jax.custom_vjp
def low(v):
    return lax.optimization_barrier(v.astype(jnp.bfloat16)).astype(jnp.float32)

@jax.custom_vjp
def low_back(v):
    return v

def low_keep(v):
    return (low(v), None)

def low_pass(kept, grad):
    return (grad,)

def back_keep(v):
    return (v, None)

def back_low(kept, grad):
    return (low(grad),)
low.defvjp(low_keep, low_pass)
low_back.defvjp(back_keep, back_low)
EPSILON = 1e-05
NEGATIVE = -1e+30

def rope_tables(length):
    halfwidth = ROT // 2
    positions = jnp.arange(length).astype(jnp.float32)
    frequency = 10000.0 ** (-jnp.arange(halfwidth).astype(jnp.float32) / halfwidth)
    angles = positions[:, None] * frequency[None, :]
    return (jnp.cos(angles)[:, None, :], jnp.sin(angles)[:, None, :])

def rotate(tensor, cosine, sines):
    halfwidth = ROT // 2
    lower_half = tensor[..., :halfwidth]
    upper_half = tensor[..., halfwidth:ROT]
    return jnp.concatenate([lower_half * cosine - upper_half * sines, upper_half * cosine + lower_half * sines, tensor[..., ROT:]], axis=-1)

def normalize(values):
    centre = values - lax.optimization_barrier(jnp.mean(values, -1, keepdims=True))
    rsigma = lax.rsqrt(lax.optimization_barrier(jnp.mean(centre * centre, -1, keepdims=True)) + EPSILON)
    return centre * rsigma

def layer(hidden_in, w_qkv, b_qkv, w_attn_out, w_up, b_up, w_down, vectors):
    highest = lax.Precision.HIGHEST
    length = hidden_in.shape[0]
    model_width = hidden_in.shape[1]
    normed = normalize(hidden_in)
    first_branch_input = low(normed * vectors[0] + vectors[1])
    second_branch_input = low(normed * vectors[2] + vectors[3])
    projected = jnp.dot(first_branch_input, w_qkv.reshape(model_width, 3 * model_width), precision=highest) + b_qkv.reshape(3 * model_width)
    projected = low_back(projected).reshape(length, 3, HEADS, HD)
    cosine, sines = rope_tables(length)
    queries = low(rotate(projected[:, 0], cosine, sines))
    keys_rot = low(rotate(projected[:, 1], cosine, sines))
    values_in = low(projected[:, 2])
    scores = low_back(jnp.einsum('qhe,khe->hqk', queries, keys_rot, precision=highest) * HD ** (-0.5))
    positions = jnp.arange(length)
    causal_mask = positions[None, :] <= positions[:, None]
    scores = jnp.where(causal_mask[None], scores, NEGATIVE)
    largest = lax.optimization_barrier(jnp.max(scores, -1, keepdims=True))
    weights = jnp.exp(scores - largest)
    weights = weights / lax.optimization_barrier(jnp.sum(weights, -1, keepdims=True))
    attended = jnp.einsum('hqk,khe->qhe', low(weights), values_in, precision=highest).reshape(length, model_width)
    attended = low(low_back(attended))
    attention = jnp.dot(attended, w_attn_out, precision=highest)
    hidden_pre = low_back(jnp.dot(second_branch_input, w_up, precision=highest) + b_up)
    gelu_hidden_output = low(jax.nn.gelu(hidden_pre, approximate=False))
    feedforward = jnp.dot(gelu_hidden_output, w_down, precision=highest)
    return hidden_in + attention + feedforward + vectors[4]

def reference(inputs, cotangent, w_qkv, b_qkv, w_attn_out, w_up, b_up, w_down, vectors):
    params = tuple((argument.astype(jnp.float32) for argument in (w_qkv, b_qkv, w_attn_out, w_up, b_up, w_down, vectors)))

    def one_sequence(running, couple):
        sequence_in, sequence_grad = couple
        result, pullback = jax.vjp(layer, sequence_in.astype(jnp.float32), *params)
        grads = pullback(sequence_grad.astype(jnp.float32))
        running = tuple((before + fresh for before, fresh in zip(running, grads[1:])))
        return (running, (result.astype(jnp.bfloat16), grads[0].astype(jnp.bfloat16)))
    zeros = tuple((jnp.zeros_like(argument) for argument in params))
    running, (outputs, input_grads) = lax.scan(one_sequence, zeros, (inputs, cotangent))
    return (outputs, input_grads, running[0], running[1], running[2], running[3], running[4], running[5], running[6])
```

```python
import functools

import jax
import jax.numpy as jnp
from jax import lax
from jax.experimental import pallas as pl
from jax.experimental.pallas import tpu as pltpu
from jax.sharding import PartitionSpec as P

HD = 64
ROT = 16
EPSILON = 1e-05
NEGATIVE = -1e30
TILE = 256
LANES = 128
F32 = jnp.float32
BF16 = jnp.bfloat16


def padded(width):
    return -(-width // LANES) * LANES


def rotary_tables(length, columns):
    half = ROT // 2
    positions = jnp.arange(length).astype(F32)
    frequency = 10000.0 ** (-jnp.arange(half).astype(F32) / half)
    angles = positions[:, None] * frequency[None, :]
    cosine, sine = jnp.cos(angles), jnp.sin(angles)
    zero = jnp.zeros_like(sine)
    rest = jnp.zeros((length, HD - ROT), F32)
    own = jnp.concatenate([cosine, cosine, rest + 1.0], 1)
    later = jnp.concatenate([-sine, zero, rest], 1)
    earlier = jnp.concatenate([zero, sine, rest], 1)
    return jnp.stack([jnp.tile(t, (1, columns // HD)) for t in (own, later, earlier)])


def dot(a, b, left, right):
    return lax.dot_general(a, b, (((left,), (right,)), ((), ())), preferred_element_type=F32)


def layer_kernel(first_call, heads, hid, *refs):
    if first_call:
        xg, w, vec, bu, bq, tab, both, gw, gs = refs[:9]
        refs = refs[9:]
        gw[...] = jnp.zeros_like(gw)
        gs[...] = jnp.zeros_like(gs)
    else:
        xg, w, vec, bu, bq, tab, gw_in, gs_in, both, gw, gs = refs[:11]
        refs = refs[11:]
        gw[...] = gw_in[...]
        gs[...] = gs_in[...]
    nrm, fst, outp, sp, q, k, v, do, att, dq, dk, dv = refs
    length, width = xg.shape[1], xg.shape[2]
    local = heads * HD
    pair = 2 * local
    up = slice(0, hid)
    down = slice(hid, 2 * hid)
    qkv_at = slice(2 * hid, 2 * hid + 3 * local)
    out_start = 2 * hid + padded(3 * local)
    out_at = slice(out_start, out_start + local)
    scale = HD ** (-0.5)

    def tables(rows):
        reps = pair // LANES
        return [jnp.concatenate([tab[n, rows, :]] * reps, axis=1) for n in range(3)]

    def before(i, carry):
        rows = pl.ds(pl.multiple_of(i * TILE, TILE), TILE)
        x = xg[0, rows, :].astype(F32)
        g = xg[1, rows, :]
        centre = x - jnp.mean(x, -1, keepdims=True)
        rsigma = lax.rsqrt(jnp.mean(centre * centre, -1, keepdims=True) + EPSILON)
        normed = centre * rsigma
        nrm[rows, :] = normed
        first = (normed * vec[0:1, :] + vec[1:2, :]).astype(BF16)
        second = (normed * vec[2:3, :] + vec[3:4, :]).astype(BF16)
        fst[rows, :] = first
        projected = dot(first, w[:, qkv_at], 1, 0) + bq[...]
        qk = projected[:, :pair]
        own, later, earlier = tables(rows)
        qk = qk * own + pltpu.roll(qk, pair - ROT // 2, 1) * later + pltpu.roll(qk, ROT // 2, 1) * earlier
        grad_att = dot(g, w[:, out_at], 1, 0)
        for h in range(heads):
            q[h, rows, :] = (qk[:, h * HD : (h + 1) * HD].astype(BF16).astype(F32) * scale).astype(BF16)
            k[h, rows, :] = qk[:, local + h * HD : local + (h + 1) * HD].astype(BF16)
            v[h, rows, :] = projected[:, pair + h * HD : pair + (h + 1) * HD].astype(BF16)
            do[h, rows, :] = grad_att[:, h * HD : (h + 1) * HD].astype(BF16)
        hidden = dot(second, w[:, up], 1, 0) + bu[...]
        cumulative = 0.5 * (1.0 + lax.erf(hidden * 0.7071067811865476))
        slope = cumulative + hidden * (jnp.exp(-0.5 * hidden * hidden) * 0.3989422804014327)
        act = (hidden * cumulative).astype(BF16)
        grad_pre32 = dot(g, w[:, down], 1, 0) * slope
        grad_pre = grad_pre32.astype(BF16)
        outp[rows, :] = dot(act, w[:, down], 1, 1)
        gw[:, down] += dot(g, act, 0, 0)
        gw[:, up] += dot(second, grad_pre, 0, 0)
        grad_second = dot(grad_pre, w[:, up], 1, 1)
        sp[rows, :] = grad_second * vec[2:3, :]
        gs[2:3, :width] += jnp.sum(grad_second * normed, 0, keepdims=True)
        gs[3:4, :width] += jnp.sum(grad_second, 0, keepdims=True)
        gs[4:5, :hid] += jnp.sum(grad_pre.astype(F32), 0, keepdims=True)
        return carry

    lax.fori_loop(0, length // TILE, before, 0)

    def head(h, carry):
        dk[h] = jnp.zeros((length, HD), F32)
        dv[h] = jnp.zeros((length, HD), F32)
        for i in range(length // TILE):
            rows = slice(i * TILE, (i + 1) * TILE)
            n = (i + 1) * TILE
            qi, doi = q[h, rows, :], do[h, rows, :]
            keys, values = k[h, :n, :], v[h, :n, :]
            scores = dot(qi, keys, 1, 1)
            column = lax.broadcasted_iota(jnp.int32, (TILE, n), 1)
            row = lax.broadcasted_iota(jnp.int32, (TILE, n), 0) + i * TILE
            scores = jnp.where(column <= row, scores, NEGATIVE)
            e = jnp.exp(scores - jnp.max(scores, -1, keepdims=True))
            probs = e * (1.0 / jnp.sum(e, -1, keepdims=True))
            low = probs.astype(BF16)
            att[h, rows, :] = dot(low, values, 1, 0).astype(BF16)
            grad_probs = dot(doi, values, 1, 1)
            inner = jnp.sum(probs * grad_probs, -1, keepdims=True)
            grad_scores = (probs * (grad_probs - inner)).astype(BF16)
            dq[h, rows, :] = dot(grad_scores, keys, 1, 0) * scale
            dk[h, :n, :] += dot(grad_scores, qi, 0, 0)
            dv[h, :n, :] += dot(low, doi, 0, 0)
        return carry

    lax.fori_loop(0, heads, head, 0)

    def after(i, carry):
        rows = pl.ds(pl.multiple_of(i * TILE, TILE), TILE)
        qk = jnp.concatenate([r[h, rows, :] for r in (dq, dk) for h in range(heads)], axis=1)
        own, later, earlier = tables(rows)
        qk = qk * own - pltpu.roll(qk, pair - ROT // 2, 1) * later - pltpu.roll(qk, ROT // 2, 1) * earlier
        grad = jnp.concatenate([qk] + [dv[h, rows, :] for h in range(heads)], axis=1).astype(BF16)
        attended = jnp.concatenate([att[h, rows, :].astype(F32) for h in range(heads)], axis=1).astype(BF16)
        g = xg[1, rows, :]
        normed = nrm[rows, :]
        gs[5:6, : 3 * local] += jnp.sum(grad.astype(F32), 0, keepdims=True)
        gw[:, qkv_at] += dot(fst[rows, :], grad, 0, 0)
        gw[:, out_at] += dot(g, attended, 0, 0)
        grad_first = dot(grad, w[:, qkv_at], 1, 1)
        gs[0:1, :width] += jnp.sum(grad_first * normed, 0, keepdims=True)
        gs[1:2, :width] += jnp.sum(grad_first, 0, keepdims=True)
        both[0, rows, :] = (outp[rows, :] + dot(attended, w[:, out_at], 1, 1)).astype(BF16)
        both[1, rows, :] = (sp[rows, :] + grad_first * vec[0:1, :]).astype(BF16)
        return carry

    lax.fori_loop(0, length // TILE, after, 0)


def layer(xg, w, vec, bu, bq, tab, sums):
    length, width = xg.shape[1], xg.shape[2]
    hid = bu.shape[1]
    local = bq.shape[1] // 3
    heads = local // HD
    most = max(width, hid, padded(3 * local))
    operands = (xg, w, vec, bu, bq, tab) + (() if sums is None else tuple(sums))
    whole = pl.BlockSpec(memory_space=pltpu.VMEM)
    perhead = (heads, length, HD)
    macs = length * width * (4 * local + 2 * hid) * 3 + 4 * heads * length * length * HD
    return pl.pallas_call(
        functools.partial(layer_kernel, sums is None, heads, hid),
        out_shape=(
            jax.ShapeDtypeStruct((2, length, width), BF16),
            jax.ShapeDtypeStruct(w.shape, F32),
            jax.ShapeDtypeStruct((8, most), F32),
        ),
        in_specs=[whole] * len(operands),
        out_specs=(whole,) * 3,
        scratch_shapes=[
            pltpu.VMEM((length, width), F32),
            pltpu.VMEM((length, width), BF16),
            pltpu.VMEM((length, width), F32),
            pltpu.VMEM((length, width), F32),
        ]
        + [pltpu.VMEM(perhead, BF16)] * 5
        + [pltpu.VMEM(perhead, F32)] * 3,
        compiler_params=pltpu.CompilerParams(vmem_limit_bytes=60 * 1024 * 1024),
        cost_estimate=pl.CostEstimate(
            flops=2 * macs, bytes_accessed=24 * 1024 * 1024, transcendentals=2 * length * hid + heads * length * length
        ),
    )(*operands)


def local(inputs, cotangent, w_qkv, b_qkv, w_attn_out, w_up, b_up, w_down, vectors):
    tensor_pos, tensor = lax.axis_index("tensor"), lax.axis_size("tensor")
    dp_pos, dp = lax.axis_index("dp"), lax.axis_size("dp")
    sequences, _, width = inputs.shape
    share, _, lw = w_qkv.shape
    hid = w_up.shape[1]
    folds = b_up.shape[0] // share
    qkv_pad = padded(3 * lw) - 3 * lw
    out_pad = padded(lw) - lw
    small = jnp.concatenate([b_qkv, vectors, b_up.reshape(folds, share)], 0).T
    packed = jnp.concatenate(
        [
            w_up,
            w_down.T,
            w_qkv.reshape(share, 3 * lw),
            jnp.pad(small, ((0, 0), (0, qkv_pad - small.shape[1]))),
            w_attn_out.T,
            jnp.zeros((share, out_pad), BF16),
        ],
        1,
    )
    w = lax.all_gather(packed, "dp", axis=0, tiled=True)
    pairs = [
        lax.all_gather(jnp.stack([inputs[s], cotangent[s]]), "tensor", axis=1, tiled=True) for s in range(sequences)
    ]
    length = pairs[0].shape[1]
    start = 2 * hid + 3 * lw
    rows = w[:, start : start + small.shape[1]].astype(F32).T
    vector_rows = rows[3:8]
    bq = lax.dynamic_slice_in_dim(rows[:3], tensor_pos * lw, lw, 1).reshape(1, 3 * lw)
    bias_up = rows[8:].reshape(folds, dp, share).transpose(1, 0, 2).reshape(-1)
    bu = lax.dynamic_slice_in_dim(bias_up, tensor_pos * hid, hid, 0).reshape(1, hid)
    vec = jnp.concatenate([vector_rows[:4], jnp.zeros((4, width), F32)], 0)
    tab = rotary_tables(length, LANES)

    sums, scattered = None, []
    for s in range(sequences):
        both, *sums = layer(pairs[s], w, vec, bu, bq, tab, sums)
        scattered.append(lax.psum_scatter(both, "tensor", scatter_dimension=1, tiled=True))
    gw, gs = sums

    cot = cotangent.astype(F32)
    grad_bq = lax.dynamic_update_slice_in_dim(
        jnp.zeros((3, width), F32), gs[5, : 3 * lw].reshape(3, lw), tensor_pos * lw, 1
    )
    grad_bu = lax.dynamic_update_slice_in_dim(jnp.zeros((hid * tensor,), F32), gs[4, :hid], tensor_pos * hid, 0)
    grad_bu = grad_bu.reshape(dp, folds, share).transpose(1, 0, 2).reshape(folds, width)
    little = jnp.concatenate([grad_bq, gs[:4, :width], jnp.sum(cot, axis=(0, 1))[None], grad_bu], 0)
    little = lax.psum(little, ("dp", "tensor"))
    little = lax.dynamic_slice_in_dim(little, dp_pos * share, share, 1)
    shares = lax.psum_scatter(gw.astype(BF16), "dp", scatter_dimension=0, tiled=True).astype(F32)

    outputs, grads = [], []
    for s in range(sequences):
        x = inputs[s].astype(F32)
        centre = x - jnp.mean(x, -1, keepdims=True)
        rsigma = lax.rsqrt(jnp.mean(centre * centre, -1, keepdims=True) + EPSILON)
        normed = centre * rsigma
        out_sum, back = scattered[s][0].astype(F32), scattered[s][1].astype(F32)
        outputs.append((x + out_sum + vector_rows[4]).astype(BF16))
        through = rsigma * (
            back - jnp.mean(back, -1, keepdims=True) - normed * jnp.mean(back * normed, -1, keepdims=True)
        )
        grads.append((cot[s] + through).astype(BF16))
    out_start = 2 * hid + padded(3 * lw)
    return (
        jnp.stack(outputs),
        jnp.stack(grads),
        shares[:, 2 * hid : start].reshape(share, 3, lw),
        little[:3],
        shares[:, out_start : out_start + lw].T,
        shares[:, :hid],
        little[8:].reshape(-1),
        shares[:, hid : 2 * hid].T,
        little[3:8],
    )


def solution(mesh):
    placed = (
        P("dp", "tensor", None),
        P("dp", "tensor", None),
        P("dp", None, "tensor"),
        P(None, "dp"),
        P("tensor", "dp"),
        P("dp", "tensor"),
        P("dp"),
        P("tensor", "dp"),
        P(None, "dp"),
    )
    return jax.shard_map(
        local,
        mesh=mesh,
        in_specs=placed,
        out_specs=placed,
        check_vma=False,
    )
```

```python
import functools

import jax
import jax.numpy as jnp
from jax import lax
from jax.experimental import pallas as pl
from jax.experimental.pallas import tpu as pltpu
from jax.sharding import PartitionSpec as P

HD = 64
ROT = 16
EPSILON = 1e-05
NEGATIVE = -1e30
TILE = 256
LANES = 128
F32 = jnp.float32
BF16 = jnp.bfloat16


def padded(width):
    return -(-width // LANES) * LANES


def rotary_tables(length, columns):
    half = ROT // 2
    positions = jnp.arange(length).astype(F32)
    frequency = 10000.0 ** (-jnp.arange(half).astype(F32) / half)
    angles = positions[:, None] * frequency[None, :]
    cosine, sine = jnp.cos(angles), jnp.sin(angles)
    zero = jnp.zeros_like(sine)
    rest = jnp.zeros((length, HD - ROT), F32)
    own = jnp.concatenate([cosine, cosine, rest + 1.0], 1)
    later = jnp.concatenate([-sine, zero, rest], 1)
    earlier = jnp.concatenate([zero, sine, rest], 1)
    return jnp.stack([jnp.tile(t, (1, columns // HD)) for t in (own, later, earlier)])


def dot(a, b, left, right):
    return lax.dot_general(a, b, (((left,), (right,)), ((), ())), preferred_element_type=F32)


class Line:
    def __init__(self, own, target, local_sem, send_sem, recv_sem, n):
        self.own, self.target, self.n = own, target, n
        self.local_sem, self.send_sem, self.recv_sem = local_sem, send_sem, recv_sem
        self.me = lax.axis_index("tensor")

    def slot(self, j):
        block = self.own.shape[1]
        return self.target.at[:, pl.ds(pl.multiple_of(j * block, block), block), :]

    def sent(self, way, step):
        me = self.me
        j = me - (step - 1) if way == 0 else me + (step - 1)
        moves = (me < self.n - 1) & (j >= 0) if way == 0 else (me > 0) & (j < self.n)
        return moves, j, (me + 1 if way == 0 else me - 1)

    def copy(self, way, step, j, other, first):
        return pltpu.make_async_remote_copy(
            src_ref=self.own if first else self.slot(j),
            dst_ref=self.slot(j),
            send_sem=self.send_sem.at[way, step - 1],
            recv_sem=self.recv_sem.at[way, step - 1],
            device_id={"tensor": other},
            device_id_type=pl.DeviceIdType.MESH,
        )

    def launch(self, step):
        for way in (0, 1):
            moves, j, other = self.sent(way, step)

            @pl.when(moves)
            def _():
                self.copy(way, step, j, other, step == 1).start()

    def arrive(self, step):
        for way in (0, 1):
            j = self.me - step if way == 0 else self.me + step
            other = self.me - 1 if way == 0 else self.me + 1

            @pl.when(j >= 0 if way == 0 else j < self.n)
            def _():
                self.copy(way, step, j, other, False).wait_recv()

    def begin(self):
        me, barrier = self.me, pltpu.get_barrier_semaphore()
        for there, other in ((me > 0, me - 1), (me < self.n - 1, me + 1)):

            @pl.when(there)
            def _():
                pl.semaphore_signal(
                    barrier, inc=1, device_id={"tensor": other}, device_id_type=pl.DeviceIdType.MESH
                )

        ends = (me == 0) | (me == self.n - 1)

        @pl.when(ends)
        def _():
            pl.semaphore_wait(barrier, 1)

        @pl.when(jnp.logical_not(ends))
        def _():
            pl.semaphore_wait(barrier, 2)

        pltpu.make_async_copy(self.own, self.slot(me), self.local_sem).start()
        self.launch(1)
        self.step = 1

    def advance(self):
        if self.step < self.n - 1:
            self.arrive(self.step)
            self.step += 1
            self.launch(self.step)

    def finish(self):
        while self.step < self.n - 1:
            self.advance()
        self.arrive(self.step)
        for step in range(1, self.n):
            for way in (0, 1):
                moves, j, other = self.sent(way, step)

                @pl.when(moves)
                def _():
                    self.copy(way, step, j, other, step == 1).wait_send()

        pltpu.make_async_copy(self.own, self.slot(self.me), self.local_sem).wait()


def line_scratch(n):
    return [
        pltpu.SemaphoreType.DMA,
        pltpu.SemaphoreType.DMA((2, n - 1)),
        pltpu.SemaphoreType.DMA((2, n - 1)),
    ]


def gather_kernel(n, own, target, *sems):
    line = Line(own, target, *sems, n)
    line.begin()
    line.finish()


def gather(own):
    n = lax.axis_size("tensor")
    return pl.pallas_call(
        functools.partial(gather_kernel, n),
        out_shape=jax.ShapeDtypeStruct((own.shape[0], own.shape[1] * n, own.shape[2]), own.dtype),
        in_specs=[pl.BlockSpec(memory_space=pl.ANY)],
        out_specs=pl.BlockSpec(memory_space=pl.ANY),
        scratch_shapes=line_scratch(n),
        compiler_params=pltpu.CompilerParams(collective_id=0, has_side_effects=True),
        cost_estimate=pl.CostEstimate(flops=0, bytes_accessed=160 * 1024 * 1024, transcendentals=0),
    )(own)


def layer_kernel(first_call, heads, hid, n, waits, *refs):
    refs = refs[waits:]
    line = None
    if n:
        own_block, refs = refs[0], refs[1:]
        at = 9 if first_call else 11
        target, refs = refs[at], refs[:at] + refs[at + 1 :]
        line = Line(own_block, target, *refs[-3:], n)
        refs = refs[:-3]
        line.begin()
    if first_call:
        xg, w, vec, bu, bq, tab, both, gw, gs = refs[:9]
        refs = refs[9:]
        gw[...] = jnp.zeros_like(gw)
        gs[...] = jnp.zeros_like(gs)
    else:
        xg, w, vec, bu, bq, tab, gw_in, gs_in, both, gw, gs = refs[:11]
        refs = refs[11:]
        gw[...] = gw_in[...]
        gs[...] = gs_in[...]
    nrm, fst, outp, sp, q, k, v, do, att, dq, dk, dv = refs
    length, width = xg.shape[1], xg.shape[2]
    local = heads * HD
    pair = 2 * local
    up = slice(0, hid)
    down = slice(hid, 2 * hid)
    qkv_at = slice(2 * hid, 2 * hid + 3 * local)
    out_start = 2 * hid + padded(3 * local)
    out_at = slice(out_start, out_start + local)
    scale = HD ** (-0.5)

    def tables(rows):
        reps = pair // LANES
        return [jnp.concatenate([tab[n, rows, :]] * reps, axis=1) for n in range(3)]

    def before(i, carry):
        rows = pl.ds(pl.multiple_of(i * TILE, TILE), TILE)
        x = xg[0, rows, :].astype(F32)
        g = xg[1, rows, :]
        centre = x - jnp.mean(x, -1, keepdims=True)
        rsigma = lax.rsqrt(jnp.mean(centre * centre, -1, keepdims=True) + EPSILON)
        normed = centre * rsigma
        nrm[rows, :] = normed
        first = (normed * vec[0:1, :] + vec[1:2, :]).astype(BF16)
        second = (normed * vec[2:3, :] + vec[3:4, :]).astype(BF16)
        fst[rows, :] = first
        projected = dot(first, w[:, qkv_at], 1, 0) + bq[...]
        qk = projected[:, :pair]
        own, later, earlier = tables(rows)
        qk = qk * own + pltpu.roll(qk, pair - ROT // 2, 1) * later + pltpu.roll(qk, ROT // 2, 1) * earlier
        grad_att = dot(g, w[:, out_at], 1, 0)
        for h in range(heads):
            q[h, rows, :] = (qk[:, h * HD : (h + 1) * HD].astype(BF16).astype(F32) * scale).astype(BF16)
            k[h, rows, :] = qk[:, local + h * HD : local + (h + 1) * HD].astype(BF16)
            v[h, rows, :] = projected[:, pair + h * HD : pair + (h + 1) * HD].astype(BF16)
            do[h, rows, :] = grad_att[:, h * HD : (h + 1) * HD].astype(BF16)
        hidden = dot(second, w[:, up], 1, 0) + bu[...]
        cumulative = 0.5 * (1.0 + lax.erf(hidden * 0.7071067811865476))
        slope = cumulative + hidden * (jnp.exp(-0.5 * hidden * hidden) * 0.3989422804014327)
        act = (hidden * cumulative).astype(BF16)
        grad_pre32 = dot(g, w[:, down], 1, 0) * slope
        grad_pre = grad_pre32.astype(BF16)
        outp[rows, :] = dot(act, w[:, down], 1, 1)
        gw[:, down] += dot(g, act, 0, 0)
        gw[:, up] += dot(second, grad_pre, 0, 0)
        grad_second = dot(grad_pre, w[:, up], 1, 1)
        sp[rows, :] = grad_second * vec[2:3, :]
        gs[2:3, :width] += jnp.sum(grad_second * normed, 0, keepdims=True)
        gs[3:4, :width] += jnp.sum(grad_second, 0, keepdims=True)
        gs[4:5, :hid] += jnp.sum(grad_pre.astype(F32), 0, keepdims=True)
        return carry

    lax.fori_loop(0, length // TILE, before, 0)
    if line:
        line.advance()

    def head(h, carry):
        dk[h] = jnp.zeros((length, HD), F32)
        dv[h] = jnp.zeros((length, HD), F32)
        for i in range(length // TILE):
            rows = slice(i * TILE, (i + 1) * TILE)
            n = (i + 1) * TILE
            qi, doi = q[h, rows, :], do[h, rows, :]
            keys, values = k[h, :n, :], v[h, :n, :]
            scores = dot(qi, keys, 1, 1)
            column = lax.broadcasted_iota(jnp.int32, (TILE, n), 1)
            row = lax.broadcasted_iota(jnp.int32, (TILE, n), 0) + i * TILE
            scores = jnp.where(column <= row, scores, NEGATIVE)
            e = jnp.exp(scores - jnp.max(scores, -1, keepdims=True))
            probs = e * (1.0 / jnp.sum(e, -1, keepdims=True))
            low = probs.astype(BF16)
            att[h, rows, :] = dot(low, values, 1, 0).astype(BF16)
            grad_probs = dot(doi, values, 1, 1)
            inner = jnp.sum(probs * grad_probs, -1, keepdims=True)
            grad_scores = (probs * (grad_probs - inner)).astype(BF16)
            dq[h, rows, :] = dot(grad_scores, keys, 1, 0) * scale
            dk[h, :n, :] += dot(grad_scores, qi, 0, 0)
            dv[h, :n, :] += dot(low, doi, 0, 0)
        return carry

    lax.fori_loop(0, heads, head, 0)
    if line:
        line.advance()

    def after(i, carry):
        rows = pl.ds(pl.multiple_of(i * TILE, TILE), TILE)
        qk = jnp.concatenate([r[h, rows, :] for r in (dq, dk) for h in range(heads)], axis=1)
        own, later, earlier = tables(rows)
        qk = qk * own - pltpu.roll(qk, pair - ROT // 2, 1) * later - pltpu.roll(qk, ROT // 2, 1) * earlier
        grad = jnp.concatenate([qk] + [dv[h, rows, :] for h in range(heads)], axis=1).astype(BF16)
        attended = jnp.concatenate([att[h, rows, :].astype(F32) for h in range(heads)], axis=1).astype(BF16)
        g = xg[1, rows, :]
        normed = nrm[rows, :]
        gs[5:6, : 3 * local] += jnp.sum(grad.astype(F32), 0, keepdims=True)
        gw[:, qkv_at] += dot(fst[rows, :], grad, 0, 0)
        gw[:, out_at] += dot(g, attended, 0, 0)
        grad_first = dot(grad, w[:, qkv_at], 1, 1)
        gs[0:1, :width] += jnp.sum(grad_first * normed, 0, keepdims=True)
        gs[1:2, :width] += jnp.sum(grad_first, 0, keepdims=True)
        both[0, rows, :] = (outp[rows, :] + dot(attended, w[:, out_at], 1, 1)).astype(BF16)
        both[1, rows, :] = (sp[rows, :] + grad_first * vec[0:1, :]).astype(BF16)
        return carry

    lax.fori_loop(0, length // TILE, after, 0)
    if line:
        line.finish()


def layer(xg, w, vec, bu, bq, tab, sums, own, call, waits):
    length, width = xg.shape[1], xg.shape[2]
    hid = bu.shape[1]
    local = bq.shape[1] // 3
    heads = local // HD
    most = max(width, hid, padded(3 * local))
    operands = (xg, w, vec, bu, bq, tab) + (() if sums is None else tuple(sums))
    whole = pl.BlockSpec(memory_space=pltpu.VMEM)
    anywhere = pl.BlockSpec(memory_space=pl.ANY)
    n = 0 if own is None else lax.axis_size("tensor")
    remote = dict(collective_id=call, has_side_effects=True) if n else {}
    perhead = (heads, length, HD)
    macs = length * width * (4 * local + 2 * hid) * 3 + 4 * heads * length * length * HD
    return pl.pallas_call(
        functools.partial(layer_kernel, sums is None, heads, hid, n, len(waits)),
        out_shape=(
            jax.ShapeDtypeStruct((2, length, width), BF16),
            jax.ShapeDtypeStruct(w.shape, F32),
            jax.ShapeDtypeStruct((8, most), F32),
        )
        + ((jax.ShapeDtypeStruct(xg.shape, BF16),) if n else ()),
        in_specs=[anywhere] * (len(waits) + bool(n)) + [whole] * len(operands),
        out_specs=(whole,) * 3 + ((anywhere,) if n else ()),
        scratch_shapes=[
            pltpu.VMEM((length, width), F32),
            pltpu.VMEM((length, width), BF16),
            pltpu.VMEM((length, width), F32),
            pltpu.VMEM((length, width), F32),
        ]
        + [pltpu.VMEM(perhead, BF16)] * 5
        + [pltpu.VMEM(perhead, F32)] * 3
        + (line_scratch(n) if n else []),
        compiler_params=pltpu.CompilerParams(vmem_limit_bytes=60 * 1024 * 1024, **remote),
        cost_estimate=pl.CostEstimate(
            flops=2 * macs, bytes_accessed=24 * 1024 * 1024, transcendentals=2 * length * hid + heads * length * length
        ),
    )(*waits, *((own,) if n else ()), *operands)


def local(inputs, cotangent, w_qkv, b_qkv, w_attn_out, w_up, b_up, w_down, vectors):
    tensor_pos, tensor = lax.axis_index("tensor"), lax.axis_size("tensor")
    dp_pos, dp = lax.axis_index("dp"), lax.axis_size("dp")
    sequences, _, width = inputs.shape
    share, _, lw = w_qkv.shape
    hid = w_up.shape[1]
    folds = b_up.shape[0] // share
    qkv_pad = padded(3 * lw) - 3 * lw
    out_pad = padded(lw) - lw
    small = jnp.concatenate([b_qkv, vectors, b_up.reshape(folds, share)], 0).T
    packed = jnp.concatenate(
        [
            w_up,
            w_down.T,
            w_qkv.reshape(share, 3 * lw),
            jnp.pad(small, ((0, 0), (0, qkv_pad - small.shape[1]))),
            w_attn_out.T,
            jnp.zeros((share, out_pad), BF16),
        ],
        1,
    )
    w = lax.all_gather(packed, "dp", axis=0, tiled=True)
    blocks = [jnp.stack([inputs[s], cotangent[s]]) for s in range(sequences)]
    pair = gather(blocks[0])
    length = pair.shape[1]
    start = 2 * hid + 3 * lw
    rows = w[:, start : start + small.shape[1]].astype(F32).T
    vector_rows = rows[3:8]
    bq = lax.dynamic_slice_in_dim(rows[:3], tensor_pos * lw, lw, 1).reshape(1, 3 * lw)
    bias_up = rows[8:].reshape(folds, dp, share).transpose(1, 0, 2).reshape(-1)
    bu = lax.dynamic_slice_in_dim(bias_up, tensor_pos * hid, hid, 0).reshape(1, hid)
    vec = jnp.concatenate([vector_rows[:4], jnp.zeros((4, width), F32)], 0)
    tab = rotary_tables(length, LANES)

    sums, scattered = None, []
    for s in range(sequences):
        ahead = blocks[s + 1] if s + 1 < sequences else None
        both, gw, gs, *pair = layer(pair, w, vec, bu, bq, tab, sums, ahead, s + 1, scattered[: max(s - 1, 0)][-1:])
        sums, pair = (gw, gs), (pair[0] if pair else None)
        scattered.append(lax.psum_scatter(both, "tensor", scatter_dimension=1, tiled=True))

    cot = cotangent.astype(F32)
    grad_bq = lax.dynamic_update_slice_in_dim(
        jnp.zeros((3, width), F32), gs[5, : 3 * lw].reshape(3, lw), tensor_pos * lw, 1
    )
    grad_bu = lax.dynamic_update_slice_in_dim(jnp.zeros((hid * tensor,), F32), gs[4, :hid], tensor_pos * hid, 0)
    grad_bu = grad_bu.reshape(dp, folds, share).transpose(1, 0, 2).reshape(folds, width)
    little = jnp.concatenate([grad_bq, gs[:4, :width], jnp.sum(cot, axis=(0, 1))[None], grad_bu], 0)
    little = lax.psum(little, ("dp", "tensor"))
    little = lax.dynamic_slice_in_dim(little, dp_pos * share, share, 1)
    if sequences > 1:
        gw, scattered[-2] = lax.optimization_barrier((gw, scattered[-2]))
    shares = lax.psum_scatter(gw.astype(BF16), "dp", scatter_dimension=0, tiled=True).astype(F32)

    outputs, grads = [], []
    for s in range(sequences):
        x = inputs[s].astype(F32)
        centre = x - jnp.mean(x, -1, keepdims=True)
        rsigma = lax.rsqrt(jnp.mean(centre * centre, -1, keepdims=True) + EPSILON)
        normed = centre * rsigma
        out_sum, back = scattered[s][0].astype(F32), scattered[s][1].astype(F32)
        outputs.append((x + out_sum + vector_rows[4]).astype(BF16))
        through = rsigma * (
            back - jnp.mean(back, -1, keepdims=True) - normed * jnp.mean(back * normed, -1, keepdims=True)
        )
        grads.append((cot[s] + through).astype(BF16))
    out_start = 2 * hid + padded(3 * lw)
    return (
        jnp.stack(outputs),
        jnp.stack(grads),
        shares[:, 2 * hid : start].reshape(share, 3, lw),
        little[:3],
        shares[:, out_start : out_start + lw].T,
        shares[:, :hid],
        little[8:].reshape(-1),
        shares[:, hid : 2 * hid].T,
        little[3:8],
    )


def solution(mesh):
    placed = (
        P("dp", "tensor", None),
        P("dp", "tensor", None),
        P("dp", None, "tensor"),
        P(None, "dp"),
        P("tensor", "dp"),
        P("dp", "tensor"),
        P("dp"),
        P("tensor", "dp"),
        P(None, "dp"),
    )
    return jax.shard_map(
        local,
        mesh=mesh,
        in_specs=placed,
        out_specs=placed,
        check_vma=False,
    )
```
